32 devices in a mesh: dp: 1, seq: 32 (over z, y, x, core).
Axes of the slice: x: 2, y: 2, z: 4, core: 2. Of those that a mesh axis runs over, the one named last changes fastest.
Arguments:
- queries: bfloat16 [4096, 2, 16, 128], P('seq', 'dp'), may hold values from -48 to 48
- keys_in: bfloat16 [4096, 2, 16, 128], P('seq', 'dp'), may hold values from -48 to 48
- values_in: bfloat16 [4096, 2, 16, 128], P('seq', 'dp'), may hold values from -6 to 6
- pair_keys: int32 [64, 27], replicated, may hold values from -1 to 63, as said below
- out_weight: bfloat16 [2048, 1536], P('seq', 'dp'), may hold values from -0.125 to 0.125
- cotangent: bfloat16 [4096, 2, 1536], P('seq', 'dp'), may hold values from -6 to 6
Outputs:
- output: bfloat16 [4096, 2, 1536], P('seq', 'dp')
- grad_queries: bfloat16 [4096, 2, 16, 128], P('seq', 'dp')
- grad_keys: bfloat16 [4096, 2, 16, 128], P('seq', 'dp')
- grad_values: bfloat16 [4096, 2, 16, 128], P('seq', 'dp')
- weight_grad: float32 [2048, 1536], P('seq', 'dp')
The draws below stay inside these ranges and needn't reach their ends.
Inputs may be any that keep to these rules, and one draw needn't show every extreme that they name: `pair_keys`: A tile's row lists the tiles whose frame, row and column tile positions each differ from its own by at most one, itself included, in increasing order, then -1 in the remaining slots; the positions of the tiles in the 4 by 4 by 4 grid are a permutation drawn anew.
All inputs are finite; a program needn't handle non-finite values.
Results may differ from the reference program's by a relative error of at most 0.022.
Values may be sent and summed in bfloat16 or wider, within the bound.
A program may use at most 320 MiB of HBM per device.

```python
import jax
import jax.numpy as jnp
from jax import lax

D = 1536
HEADS = 16
HEAD_DIM = 128
TILE = 64
TILE_H = 4
TILE_W = 4
KMAX = 27
TOKENS = 4096
VIDEOS = 2
TILES = 64


def query_key_pair(key):
    draw_key = jax.random.fold_in(key, 17)
    key_one, key_two = jax.random.split(draw_key)
    full_shape = (TOKENS, VIDEOS, HEADS, HEAD_DIM)
    query_raw = jnp.clip(jax.random.normal(key_one, full_shape, jnp.float32), -6.0, 6.0)
    key_raw = jnp.clip(jax.random.normal(key_two, full_shape, jnp.float32), -6.0, 6.0)
    query_final = query_raw
    key_final = key_raw
    return (query_final, key_final)


def draw_queries(key, part):
    return query_key_pair(key)[0].astype(jnp.bfloat16)


def draw_keys_in(key, part):
    return query_key_pair(key)[1].astype(jnp.bfloat16)


def draw_pair_keys(key, part):
    position = jax.random.permutation(jax.random.fold_in(key, 29), TILES)
    plane = TILE_H * TILE_W
    frame_of = position // plane
    row_of = position // TILE_W % TILE_H
    col_of = position % TILE_W
    inside = (jnp.abs(frame_of[:, None] - frame_of[None, :]) <= 1) & (jnp.abs(row_of[:, None] - row_of[None, :]) <= 1) & (jnp.abs(col_of[:, None] - col_of[None, :]) <= 1)
    priority = jnp.where(inside, TILES - jnp.arange(TILES, dtype=jnp.int32)[None, :], 0).astype(jnp.int32)
    best_vals, best_index = lax.top_k(priority, KMAX)
    return jnp.where(best_vals > 0, best_index, -1).astype(jnp.int32)


def block_scale(own_key, dims, pieces, smallest, top_value):
    loudness, own = 1.0, jax.random.fold_in(own_key, 6)
    for dim, blocks in pieces:
        steps = jnp.exp(jax.random.uniform(jax.random.fold_in(own, dim), (blocks,), jnp.float32, smallest / len(pieces), top_value / len(pieces)))
        loudness = loudness * jnp.repeat(steps, dims[dim] // blocks).reshape([-1 if axis == dim else 1 for axis in range(len(dims))])
    return loudness


def scatter_about(own_key, extent, deviation, reach, shards=(), kind=jnp.bfloat16):
    drawn = jax.random.normal(own_key, extent, jnp.float32) * deviation
    if len(shards) > 0:
        drawn = block_scale(own_key, extent, shards, -0.22, 0.18) * drawn
    return jnp.clip(drawn, min=-reach, max=reach).astype(kind)


def setup_inputs(seed: int = 0) -> dict:
    key_of = jax.random.split(jax.random.key(seed), 7)
    queries = draw_queries(jax.random.fold_in(key_of[6], 71), 0)
    keys_in = draw_keys_in(jax.random.fold_in(key_of[6], 71), 0)
    values_in = scatter_about(key_of[2], (TOKENS, VIDEOS, HEADS, HEAD_DIM), 1.0, 6.0, ((0, 32),))
    pair_keys = draw_pair_keys(jax.random.fold_in(key_of[6], 71), 0)
    out_weight = scatter_about(key_of[4], (HEADS * HEAD_DIM, D), (HEADS * HEAD_DIM) ** -0.5, 0.125, ((0, 32),))
    cotangent = scatter_about(key_of[5], (TOKENS, VIDEOS, D), 1.0, 6.0, ((0, 32),))
    return {"queries": queries, "keys_in": keys_in, "values_in": values_in, "pair_keys": pair_keys, "out_weight": out_weight, "cotangent": cotangent}


def rounded(values):
    return lax.optimization_barrier(values.astype(jnp.bfloat16)).astype(jnp.float32)


def block_scores(query_block, key_block, key_index):
    score_scale = HEAD_DIM ** -0.5
    usable = key_index >= 0
    scores = jnp.einsum("qad,qkbd->qakb", query_block, key_block) * score_scale
    return jnp.where(usable[:, None, :, None], scores, -jnp.inf)


def unit_forward(query_unit, key_unit, value_unit, pair_keys):
    key_tiles = key_unit.astype(jnp.float32).reshape(TILES, TILE, HEAD_DIM)
    value_tiles = value_unit.astype(jnp.float32).reshape(TILES, TILE, HEAD_DIM)
    query_blocks = query_unit.astype(jnp.float32).reshape(TILES // 8, 8, TILE, HEAD_DIM)
    key_table = pair_keys.reshape(TILES // 8, 8, KMAX)

    def one_block(packed):
        query_block, key_index = packed
        clipped = jnp.maximum(key_index, 0)
        scores = block_scores(query_block, key_tiles[clipped], key_index)
        row_max = jnp.max(scores, axis=(2, 3), keepdims=True)
        log_total = row_max + jnp.log(jnp.sum(jnp.exp(scores - row_max), axis=(2, 3), keepdims=True))
        weights = rounded(jnp.exp(scores - log_total))
        result = jnp.einsum("qakb,qkbd->qad", weights, value_tiles[clipped])
        return result.astype(jnp.bfloat16), log_total[:, :, 0, 0]

    unit_outs, unit_sums = lax.map(one_block, (query_blocks, key_table))
    return unit_outs.reshape(TOKENS, HEAD_DIM), unit_sums.reshape(TOKENS)


def unit_backward(query_unit, key_unit, value_unit, out_unit, log_unit, grad_unit, pair_keys):
    score_scale = HEAD_DIM ** -0.5
    grad_float = grad_unit.astype(jnp.float32)
    row_delta = jnp.sum(grad_float * out_unit.astype(jnp.float32), axis=-1)
    key_tiles = key_unit.astype(jnp.float32).reshape(TILES, TILE, HEAD_DIM)
    value_tiles = value_unit.astype(jnp.float32).reshape(TILES, TILE, HEAD_DIM)
    blocks = TILES // 8
    packed = (query_unit.astype(jnp.float32).reshape(blocks, 8, TILE, HEAD_DIM),
              grad_float.reshape(blocks, 8, TILE, HEAD_DIM),
              row_delta.reshape(blocks, 8, TILE),
              log_unit.reshape(blocks, 8, TILE),
              pair_keys.reshape(blocks, 8, KMAX))

    def one_block(carry, inputs):
        key_acc, value_acc = carry
        query_block, grad_block, delta_block, log_block, key_index = inputs
        clipped = jnp.maximum(key_index, 0)
        key_block = key_tiles[clipped]
        value_block = value_tiles[clipped]
        scores = block_scores(query_block, key_block, key_index)
        prob_full = jnp.exp(scores - log_block[:, :, None, None])
        weights = rounded(prob_full)
        value_part = jnp.einsum("qakb,qad->qkbd", weights, grad_block)
        grad_probs = jnp.einsum("qad,qkbd->qakb", grad_block, value_block)
        grad_scores = rounded(prob_full * (grad_probs - delta_block[:, :, None, None]) * score_scale)
        query_grad = jnp.einsum("qakb,qkbd->qad", grad_scores, key_block).astype(jnp.bfloat16)
        key_part = jnp.einsum("qakb,qad->qkbd", grad_scores, query_block)
        key_acc = key_acc.at[clipped].add(key_part)
        value_acc = value_acc.at[clipped].add(value_part)
        return (key_acc, value_acc), query_grad

    empty_acc = jnp.zeros((TILES, TILE, HEAD_DIM), jnp.float32)
    (key_acc, value_acc), query_grads = lax.scan(one_block, (empty_acc, empty_acc), packed)
    return (query_grads.reshape(TOKENS, HEAD_DIM),
            key_acc.reshape(TOKENS, HEAD_DIM).astype(jnp.bfloat16),
            value_acc.reshape(TOKENS, HEAD_DIM).astype(jnp.bfloat16))


def to_units(values):
    return jnp.transpose(values, (1, 2, 0, 3)).reshape(VIDEOS * HEADS, TOKENS, HEAD_DIM)


def from_units(values):
    return jnp.transpose(values.reshape(VIDEOS, HEADS, TOKENS, HEAD_DIM), (2, 0, 1, 3))


def reference(queries, keys_in, values_in, pair_keys, out_weight, cotangent):
    query_units = to_units(queries)
    key_units = to_units(keys_in)
    value_units = to_units(values_in)
    out_units, log_units = lax.map(lambda packed: unit_forward(packed[0], packed[1], packed[2], pair_keys),
                                   (query_units, key_units, value_units))
    attention = from_units(out_units).reshape(TOKENS * VIDEOS, HEADS * HEAD_DIM)
    cot_rows = cotangent.reshape(TOKENS * VIDEOS, D)
    output = jnp.dot(attention, out_weight, preferred_element_type=jnp.float32).astype(jnp.bfloat16)
    weight_grad = jnp.dot(attention.T, cot_rows, preferred_element_type=jnp.float32)
    grad_attention = jnp.dot(cot_rows, out_weight.T, preferred_element_type=jnp.float32).astype(jnp.bfloat16)
    grad_units = to_units(grad_attention.reshape(TOKENS, VIDEOS, HEADS, HEAD_DIM))
    grad_q, grad_k, grad_v = lax.map(
        lambda packed: unit_backward(packed[0], packed[1], packed[2], packed[3], packed[4], packed[5], pair_keys),
        (query_units, key_units, value_units, out_units, log_units, grad_units))
    return (output.reshape(TOKENS, VIDEOS, D), from_units(grad_q), from_units(grad_k),
            from_units(grad_v), weight_grad)
```

```python
import functools

import jax
import jax.numpy as jnp
from jax import lax
from jax.experimental import pallas as pl
from jax.experimental.pallas import tpu as pltpu
from jax.sharding import PartitionSpec as P


LOG2E = 1.4426950408889634
HIDDEN = -1e30
CHUNK_TILES = 4


def group_tables(pair_keys, tile_len):
    tile_count, slot_count = pair_keys.shape
    group_count = 8
    group_size = 8
    padded = -(-slot_count // CHUNK_TILES) * CHUNK_TILES
    tile_ids = jnp.arange(tile_count, dtype=jnp.int32)
    counts = jnp.sum((pair_keys >= 0).astype(jnp.int32), axis=1)
    is_corner = counts == group_size
    before = (tile_ids[None, :] < tile_ids[:, None]) & is_corner[None, :]
    rank = jnp.sum(before.astype(jnp.int32), axis=1)
    pick = (rank[None, :] == jnp.arange(group_count, dtype=jnp.int32)[:, None]) & is_corner[None, :]
    query_tiles = jnp.sum(jnp.where(pick[:, :, None], pair_keys[None, :, :group_size], 0), axis=1)
    member = query_tiles[:, :, None] == tile_ids[None, None, :]
    inner = jnp.any(member, axis=1) & (counts == slot_count)[None, :]
    key_tiles = jnp.sum(jnp.where(inner[:, :, None], pair_keys[None], 0), axis=1)
    rows = jnp.sum(jnp.where(member[..., None], pair_keys[None, None], 0), axis=2)
    seen = jnp.any(rows[:, None, :, :] == key_tiles[:, :, None, None], axis=3)
    bias = jnp.where(seen, 0.0, HIDDEN).astype(jnp.float32)
    bias = jnp.pad(bias, ((0, 0), (0, padded - slot_count), (0, 0)), constant_values=HIDDEN)
    bias = jnp.repeat(bias, tile_len, axis=2)
    key_tiles = jnp.pad(key_tiles, ((0, 0), (0, padded - slot_count)))
    return query_tiles, key_tiles, bias


def gather_tiles(table, group, source, target, count, tile_len):
    for slot in range(count):
        start = pl.multiple_of(table[group, slot] * tile_len, tile_len)
        target[slot * tile_len : (slot + 1) * tile_len, :] = source[pl.ds(start, tile_len), :]


def dot_nt(left, right):
    return lax.dot_general(
        left, right, (((1,), (1,)), ((), ())), preferred_element_type=jnp.float32
    )


def dot_tn(left, right):
    return lax.dot_general(
        left, right, (((0,), (0,)), ((), ())), preferred_element_type=jnp.float32
    )


def add_bias(scores, bias_rows, tile_len):
    keys, cols = scores.shape
    split = scores.reshape(keys // tile_len, tile_len, cols) + bias_rows[:, None, :]
    return split.reshape(keys, cols)


def forward_kernel(
    tile_len, q_table, k_table, q_ref, k_ref, v_ref, bias_ref, o_ref, lse_ref,
    q_buf, k_buf, v_buf, s_buf,
):
    group = pl.program_id(0)
    query_count = q_buf.shape[0] // tile_len
    key_count = k_buf.shape[0] // tile_len
    gather_tiles(q_table, group, q_ref, q_buf, query_count, tile_len)
    gather_tiles(k_table, group, k_ref, k_buf, key_count, tile_len)
    gather_tiles(k_table, group, v_ref, v_buf, key_count, tile_len)
    head_size = q_buf.shape[1]
    factor = head_size ** (-0.5) * LOG2E
    step = CHUNK_TILES * tile_len
    chunks = key_count // CHUNK_TILES
    queries = q_buf[...]
    top = None
    for part in range(chunks):
        scores = dot_nt(k_buf[part * step : (part + 1) * step, :], queries) * factor
        bias_rows = bias_ref[0, part * CHUNK_TILES : (part + 1) * CHUNK_TILES, :]
        scores = add_bias(scores, bias_rows, tile_len)
        s_buf[part * step : (part + 1) * step, :] = scores
        part_top = jnp.max(scores, axis=0, keepdims=True)
        top = part_top if top is None else jnp.maximum(top, part_top)
    total = jnp.zeros_like(top)
    result = jnp.zeros((head_size, queries.shape[0]), jnp.float32)
    for part in range(chunks):
        probs = jnp.exp2(s_buf[part * step : (part + 1) * step, :] - top)
        total = total + jnp.sum(probs, axis=0, keepdims=True)
        values = v_buf[part * step : (part + 1) * step, :]
        result = result + dot_tn(values, probs.astype(jnp.bfloat16))
    lse_ref[0] = top + jnp.log2(total)
    out = jnp.transpose(result / total).astype(jnp.bfloat16)
    for slot in range(query_count):
        start = pl.multiple_of(q_table[group, slot] * tile_len, tile_len)
        o_ref[pl.ds(start, tile_len), :] = out[slot * tile_len : (slot + 1) * tile_len, :]


def backward_kernel(
    tile_len, q_table, k_table, q_ref, k_ref, v_ref, o_ref, g_ref, bias_ref, lse_ref,
    dq_ref, dk_ref, dv_ref, q_buf, k_buf, v_buf, o_buf, g_buf, k_acc, v_acc,
):
    group = pl.program_id(0)
    query_count = q_buf.shape[0] // tile_len
    key_count = k_buf.shape[0] // tile_len

    @pl.when(group == 0)
    def _():
        k_acc[...] = jnp.zeros_like(k_acc)
        v_acc[...] = jnp.zeros_like(v_acc)

    gather_tiles(q_table, group, q_ref, q_buf, query_count, tile_len)
    gather_tiles(q_table, group, o_ref, o_buf, query_count, tile_len)
    gather_tiles(q_table, group, g_ref, g_buf, query_count, tile_len)
    gather_tiles(k_table, group, k_ref, k_buf, key_count, tile_len)
    gather_tiles(k_table, group, v_ref, v_buf, key_count, tile_len)
    head_size = q_buf.shape[1]
    scale = head_size ** (-0.5)
    step = CHUNK_TILES * tile_len
    chunks = key_count // CHUNK_TILES
    queries = q_buf[...]
    grads = g_buf[...]
    products = grads.astype(jnp.float32) * o_buf[...].astype(jnp.float32)
    delta = jnp.sum(jnp.transpose(products), axis=0, keepdims=True)
    log_total = lse_ref[0]
    query_grad = jnp.zeros((head_size, queries.shape[0]), jnp.float32)
    for part in range(chunks):
        keys = k_buf[part * step : (part + 1) * step, :]
        values = v_buf[part * step : (part + 1) * step, :]
        bias_rows = bias_ref[0, part * CHUNK_TILES : (part + 1) * CHUNK_TILES, :] - log_total
        scores = dot_nt(keys, queries) * (scale * LOG2E)
        probs = jnp.exp2(add_bias(scores, bias_rows, tile_len))
        grad_probs = dot_nt(values, grads)
        grad_scores = (probs * ((grad_probs - delta) * scale)).astype(jnp.bfloat16)
        value_part = jnp.dot(
            probs.astype(jnp.bfloat16), grads, preferred_element_type=jnp.float32
        )
        key_part = jnp.dot(grad_scores, queries, preferred_element_type=jnp.float32)
        query_grad = query_grad + dot_tn(keys, grad_scores)
        for slot in range(CHUNK_TILES):
            tile = k_table[group, part * CHUNK_TILES + slot]
            start = pl.multiple_of(tile * tile_len, tile_len)
            here = slice(slot * tile_len, (slot + 1) * tile_len)
            k_acc[pl.ds(start, tile_len), :] += key_part[here, :]
            v_acc[pl.ds(start, tile_len), :] += value_part[here, :]
    out = jnp.transpose(query_grad).astype(jnp.bfloat16)
    for slot in range(query_count):
        start = pl.multiple_of(q_table[group, slot] * tile_len, tile_len)
        dq_ref[pl.ds(start, tile_len), :] = out[slot * tile_len : (slot + 1) * tile_len, :]

    @pl.when(group == pl.num_programs(0) - 1)
    def _():
        dk_ref[...] = k_acc[...].astype(jnp.bfloat16)
        dv_ref[...] = v_acc[...].astype(jnp.bfloat16)


def whole_spec(shape):
    return pl.BlockSpec(shape, lambda group, q_table, k_table: (0, 0))


def group_spec(shape):
    return pl.BlockSpec((1,) + shape, lambda group, q_table, k_table: (group, 0, 0))


def unit_forward(query_unit, key_unit, value_unit, tables, tile_len):
    query_tiles, key_tiles, bias = tables
    tokens_all, head_size = query_unit.shape
    groups, group_size = query_tiles.shape
    rows, cols = key_tiles.shape[1] * tile_len, group_size * tile_len
    whole = whole_spec((tokens_all, head_size))
    return pl.pallas_call(
        functools.partial(forward_kernel, tile_len),
        out_shape=(
            jax.ShapeDtypeStruct((tokens_all, head_size), jnp.bfloat16),
            jax.ShapeDtypeStruct((groups, 1, cols), jnp.float32),
        ),
        grid_spec=pltpu.PrefetchScalarGridSpec(
            num_scalar_prefetch=2,
            grid=(groups,),
            in_specs=[whole, whole, whole, group_spec(bias.shape[1:])],
            out_specs=(whole, group_spec((1, cols))),
            scratch_shapes=[
                pltpu.VMEM((cols, head_size), jnp.bfloat16),
                pltpu.VMEM((rows, head_size), jnp.bfloat16),
                pltpu.VMEM((rows, head_size), jnp.bfloat16),
                pltpu.VMEM((rows, cols), jnp.float32),
            ],
        ),
        compiler_params=pltpu.CompilerParams(vmem_limit_bytes=40 * 2**20),
        cost_estimate=pl.CostEstimate(
            flops=4 * groups * rows * cols * head_size * 2,
            bytes_accessed=8 * tokens_all * head_size,
            transcendentals=groups * rows * cols,
        ),
    )(query_tiles, key_tiles, query_unit, key_unit, value_unit, bias)


def unit_backward(query_unit, key_unit, value_unit, out_unit, log_unit, grad_unit, tables, tile_len):
    query_tiles, key_tiles, bias = tables
    tokens_all, head_size = query_unit.shape
    groups, group_size = query_tiles.shape
    rows, cols = key_tiles.shape[1] * tile_len, group_size * tile_len
    whole = whole_spec((tokens_all, head_size))
    shape = jax.ShapeDtypeStruct((tokens_all, head_size), jnp.bfloat16)
    return pl.pallas_call(
        functools.partial(backward_kernel, tile_len),
        out_shape=(shape, shape, shape),
        grid_spec=pltpu.PrefetchScalarGridSpec(
            num_scalar_prefetch=2,
            grid=(groups,),
            in_specs=[whole] * 5 + [group_spec(bias.shape[1:]), group_spec((1, cols))],
            out_specs=(whole, whole, whole),
            scratch_shapes=[
                pltpu.VMEM((cols, head_size), jnp.bfloat16),
                pltpu.VMEM((rows, head_size), jnp.bfloat16),
                pltpu.VMEM((rows, head_size), jnp.bfloat16),
                pltpu.VMEM((cols, head_size), jnp.bfloat16),
                pltpu.VMEM((cols, head_size), jnp.bfloat16),
                pltpu.VMEM((tokens_all, head_size), jnp.float32),
                pltpu.VMEM((tokens_all, head_size), jnp.float32),
            ],
        ),
        compiler_params=pltpu.CompilerParams(vmem_limit_bytes=48 * 2**20),
        cost_estimate=pl.CostEstimate(
            flops=10 * groups * rows * cols * head_size * 2,
            bytes_accessed=16 * tokens_all * head_size,
            transcendentals=groups * rows * cols,
        ),
    )(query_tiles, key_tiles, query_unit, key_unit, value_unit, out_unit, grad_unit, bias, log_unit)


def local(queries, keys_in, values_in, pair_keys, out_weight, cotangent):
    tok_rows, local_videos, head_count, head_size = queries.shape
    unit_total = local_videos * head_count
    seq_size = lax.axis_size("seq")
    units_here = unit_total // seq_size
    row_count = tok_rows * local_videos
    width_heads = head_count * head_size
    split_shape = (tok_rows, seq_size, units_here, head_size)
    query_all = lax.all_to_all(
        queries.reshape(split_shape), "seq", split_axis=1, concat_axis=0, tiled=True
    )
    key_all = lax.all_to_all(
        keys_in.reshape(split_shape), "seq", split_axis=1, concat_axis=0, tiled=True
    )
    value_all = lax.all_to_all(
        values_in.reshape(split_shape), "seq", split_axis=1, concat_axis=0, tiled=True
    )
    tile_len = query_all.shape[0] // pair_keys.shape[0]
    tables = group_tables(pair_keys, tile_len)
    query_unit, key_unit, value_unit = query_all[:, 0, 0], key_all[:, 0, 0], value_all[:, 0, 0]
    result, log_total = unit_forward(query_unit, key_unit, value_unit, tables, tile_len)
    heads_out = result[:, None, None]
    attn_tok = lax.all_to_all(heads_out, "seq", split_axis=0, concat_axis=1, tiled=True)
    attn_rows = attn_tok.reshape(row_count, width_heads)
    cot_rows = cotangent.reshape(row_count, cotangent.shape[2])
    weight_cols = lax.all_gather(out_weight, "dp", axis=1, tiled=True)
    weight_full = lax.all_gather(weight_cols, "seq", axis=0, tiled=True)
    projected = jnp.dot(attn_rows, weight_full, preferred_element_type=jnp.float32)
    grad_attention = jnp.einsum(
        "rd,cd->rc", cot_rows, weight_full, preferred_element_type=jnp.float32
    ).astype(jnp.bfloat16)
    output = projected.astype(jnp.bfloat16).reshape(tok_rows, local_videos, cotangent.shape[2])
    by_rows = lax.psum_scatter(
        jnp.einsum("rc,rd->cd", attn_rows, cot_rows, preferred_element_type=jnp.float32).astype(
            jnp.bfloat16
        ),
        "seq",
        scatter_dimension=0,
        tiled=True,
    )
    weight_grad = lax.psum_scatter(by_rows, "dp", scatter_dimension=1, tiled=True).astype(
        jnp.float32
    )
    grad_heads = lax.all_to_all(
        grad_attention.reshape(split_shape), "seq", split_axis=1, concat_axis=0, tiled=True
    )
    grad_q, grad_k, grad_v = unit_backward(
        query_unit, key_unit, value_unit, result, log_total, grad_heads[:, 0, 0], tables, tile_len
    )
    query_parts = [grad_q]
    key_parts = [grad_k]
    value_parts = [grad_v]
    grad_query_tok, grad_key_tok, grad_value_tok = (
        lax.all_to_all(
            jnp.stack(query_parts, 1)[:, None], "seq", split_axis=0, concat_axis=1, tiled=True
        ),
        lax.all_to_all(
            jnp.stack(key_parts, 1)[:, None], "seq", split_axis=0, concat_axis=1, tiled=True
        ),
        lax.all_to_all(
            jnp.stack(value_parts, 1)[:, None], "seq", split_axis=0, concat_axis=1, tiled=True
        ),
    )
    full_shape = (tok_rows, local_videos, head_count, head_size)
    return (
        output,
        grad_query_tok.reshape(full_shape),
        grad_key_tok.reshape(full_shape),
        grad_value_tok.reshape(full_shape),
        weight_grad,
    )


def solution(mesh):
    placed = (
        P("seq", "dp", None, None),
        P("seq", "dp", None, None),
        P("seq", "dp", None, None),
        P(),
        P("seq", "dp"),
        P("seq", "dp", None),
    )
    return jax.shard_map(
        local,
        mesh=mesh,
        in_specs=placed,
        out_specs=(
            P("seq", "dp", None),
            P("seq", "dp", None, None),
            P("seq", "dp", None, None),
            P("seq", "dp", None, None),
            P("seq", "dp"),
        ),
        check_vma=False,
    )
```

```python
import functools

import jax
import jax.numpy as jnp
from jax import lax
from jax.experimental import pallas as pl
from jax.experimental.pallas import tpu as pltpu
from jax.sharding import PartitionSpec as P


LOG2E = 1.4426950408889634
HIDDEN = -1e30
CHUNK_TILES = 4


def group_tables(pair_keys, tile_len):
    tile_count, slot_count = pair_keys.shape
    group_count = 8
    group_size = 8
    padded = -(-slot_count // CHUNK_TILES) * CHUNK_TILES
    tile_ids = jnp.arange(tile_count, dtype=jnp.int32)
    counts = jnp.sum((pair_keys >= 0).astype(jnp.int32), axis=1)
    is_corner = counts == group_size
    before = (tile_ids[None, :] < tile_ids[:, None]) & is_corner[None, :]
    rank = jnp.sum(before.astype(jnp.int32), axis=1)
    pick = (rank[None, :] == jnp.arange(group_count, dtype=jnp.int32)[:, None]) & is_corner[None, :]
    query_tiles = jnp.sum(jnp.where(pick[:, :, None], pair_keys[None, :, :group_size], 0), axis=1)
    member = query_tiles[:, :, None] == tile_ids[None, None, :]
    inner = jnp.any(member, axis=1) & (counts == slot_count)[None, :]
    key_tiles = jnp.sum(jnp.where(inner[:, :, None], pair_keys[None], 0), axis=1)
    rows = jnp.sum(jnp.where(member[..., None], pair_keys[None, None], 0), axis=2)
    seen = jnp.any(rows[:, None, :, :] == key_tiles[:, :, None, None], axis=3)
    bias = jnp.where(seen, 0.0, HIDDEN).astype(jnp.float32)
    bias = jnp.pad(bias, ((0, 0), (0, padded - slot_count), (0, 0)), constant_values=HIDDEN)
    bias = jnp.repeat(bias, tile_len, axis=2)
    key_tiles = jnp.pad(key_tiles, ((0, 0), (0, padded - slot_count)))
    return query_tiles, key_tiles, bias


def gather_tiles(table, group, source, target, count, tile_len):
    for slot in range(count):
        start = pl.multiple_of(table[group, slot] * tile_len, tile_len)
        target[slot * tile_len : (slot + 1) * tile_len, :] = source[pl.ds(start, tile_len), :]


def dot_nt(left, right):
    return lax.dot_general(
        left, right, (((1,), (1,)), ((), ())), preferred_element_type=jnp.float32
    )


def dot_tn(left, right):
    return lax.dot_general(
        left, right, (((0,), (0,)), ((), ())), preferred_element_type=jnp.float32
    )


def add_bias(scores, bias_rows, tile_len):
    keys, cols = scores.shape
    split = scores.reshape(keys // tile_len, tile_len, cols) + bias_rows[:, None, :]
    return split.reshape(keys, cols)


def forward_kernel(
    tile_len, q_table, k_table, q_ref, k_ref, v_ref, bias_ref, o_ref, lse_ref,
    q_buf, k_buf, v_buf, s_buf,
):
    group = pl.program_id(0)
    query_count = q_buf.shape[0] // tile_len
    key_count = k_buf.shape[0] // tile_len
    gather_tiles(q_table, group, q_ref, q_buf, query_count, tile_len)
    gather_tiles(k_table, group, k_ref, k_buf, key_count, tile_len)
    gather_tiles(k_table, group, v_ref, v_buf, key_count, tile_len)
    head_size = q_buf.shape[1]
    factor = head_size ** (-0.5) * LOG2E
    step = CHUNK_TILES * tile_len
    chunks = key_count // CHUNK_TILES
    queries = q_buf[...]
    top = None
    for part in range(chunks):
        scores = dot_nt(k_buf[part * step : (part + 1) * step, :], queries) * factor
        bias_rows = bias_ref[0, part * CHUNK_TILES : (part + 1) * CHUNK_TILES, :]
        scores = add_bias(scores, bias_rows, tile_len)
        s_buf[part * step : (part + 1) * step, :] = scores
        part_top = jnp.max(scores, axis=0, keepdims=True)
        top = part_top if top is None else jnp.maximum(top, part_top)
    total = jnp.zeros_like(top)
    result = jnp.zeros((head_size, queries.shape[0]), jnp.float32)
    for part in range(chunks):
        probs = jnp.exp2(s_buf[part * step : (part + 1) * step, :] - top)
        total = total + jnp.sum(probs, axis=0, keepdims=True)
        values = v_buf[part * step : (part + 1) * step, :]
        result = result + dot_tn(values, probs.astype(jnp.bfloat16))
    lse_ref[0] = top + jnp.log2(total)
    out = jnp.transpose(result / total).astype(jnp.bfloat16)
    for slot in range(query_count):
        start = pl.multiple_of(q_table[group, slot] * tile_len, tile_len)
        o_ref[pl.ds(start, tile_len), :] = out[slot * tile_len : (slot + 1) * tile_len, :]


def backward_kernel(
    tile_len, q_table, k_table, q_ref, k_ref, v_ref, o_ref, g_ref, bias_ref, lse_ref,
    dq_ref, dk_ref, dv_ref, q_buf, k_buf, v_buf, o_buf, g_buf, k_acc, v_acc,
):
    group = pl.program_id(0)
    query_count = q_buf.shape[0] // tile_len
    key_count = k_buf.shape[0] // tile_len

    @pl.when(group == 0)
    def _():
        k_acc[...] = jnp.zeros_like(k_acc)
        v_acc[...] = jnp.zeros_like(v_acc)

    gather_tiles(q_table, group, q_ref, q_buf, query_count, tile_len)
    gather_tiles(q_table, group, o_ref, o_buf, query_count, tile_len)
    gather_tiles(q_table, group, g_ref, g_buf, query_count, tile_len)
    gather_tiles(k_table, group, k_ref, k_buf, key_count, tile_len)
    gather_tiles(k_table, group, v_ref, v_buf, key_count, tile_len)
    head_size = q_buf.shape[1]
    scale = head_size ** (-0.5)
    step = CHUNK_TILES * tile_len
    chunks = key_count // CHUNK_TILES
    queries = q_buf[...]
    grads = g_buf[...]
    products = grads.astype(jnp.float32) * o_buf[...].astype(jnp.float32)
    delta = jnp.sum(jnp.transpose(products), axis=0, keepdims=True)
    log_total = lse_ref[0]
    query_grad = jnp.zeros((head_size, queries.shape[0]), jnp.float32)
    for part in range(chunks):
        keys = k_buf[part * step : (part + 1) * step, :]
        values = v_buf[part * step : (part + 1) * step, :]
        bias_rows = bias_ref[0, part * CHUNK_TILES : (part + 1) * CHUNK_TILES, :] - log_total
        scores = dot_nt(keys, queries) * (scale * LOG2E)
        probs = jnp.exp2(add_bias(scores, bias_rows, tile_len))
        grad_probs = dot_nt(values, grads)
        grad_scores = (probs * ((grad_probs - delta) * scale)).astype(jnp.bfloat16)
        value_part = jnp.dot(
            probs.astype(jnp.bfloat16), grads, preferred_element_type=jnp.float32
        )
        key_part = jnp.dot(grad_scores, queries, preferred_element_type=jnp.float32)
        query_grad = query_grad + dot_tn(keys, grad_scores)
        for slot in range(CHUNK_TILES):
            tile = k_table[group, part * CHUNK_TILES + slot]
            start = pl.multiple_of(tile * tile_len, tile_len)
            here = slice(slot * tile_len, (slot + 1) * tile_len)
            k_acc[pl.ds(start, tile_len), :] += key_part[here, :]
            v_acc[pl.ds(start, tile_len), :] += value_part[here, :]
    out = jnp.transpose(query_grad).astype(jnp.bfloat16)
    for slot in range(query_count):
        start = pl.multiple_of(q_table[group, slot] * tile_len, tile_len)
        dq_ref[pl.ds(start, tile_len), :] = out[slot * tile_len : (slot + 1) * tile_len, :]

    @pl.when(group == pl.num_programs(0) - 1)
    def _():
        dk_ref[...] = k_acc[...].astype(jnp.bfloat16)
        dv_ref[...] = v_acc[...].astype(jnp.bfloat16)


def whole_spec(shape):
    return pl.BlockSpec(shape, lambda group, q_table, k_table: (0, 0))


def group_spec(shape):
    return pl.BlockSpec((1,) + shape, lambda group, q_table, k_table: (group, 0, 0))


def unit_forward(query_unit, key_unit, value_unit, tables, tile_len):
    query_tiles, key_tiles, bias = tables
    tokens_all, head_size = query_unit.shape
    groups, group_size = query_tiles.shape
    rows, cols = key_tiles.shape[1] * tile_len, group_size * tile_len
    whole = whole_spec((tokens_all, head_size))
    return pl.pallas_call(
        functools.partial(forward_kernel, tile_len),
        out_shape=(
            jax.ShapeDtypeStruct((tokens_all, head_size), jnp.bfloat16),
            jax.ShapeDtypeStruct((groups, 1, cols), jnp.float32),
        ),
        grid_spec=pltpu.PrefetchScalarGridSpec(
            num_scalar_prefetch=2,
            grid=(groups,),
            in_specs=[whole, whole, whole, group_spec(bias.shape[1:])],
            out_specs=(whole, group_spec((1, cols))),
            scratch_shapes=[
                pltpu.VMEM((cols, head_size), jnp.bfloat16),
                pltpu.VMEM((rows, head_size), jnp.bfloat16),
                pltpu.VMEM((rows, head_size), jnp.bfloat16),
                pltpu.VMEM((rows, cols), jnp.float32),
            ],
        ),
        compiler_params=pltpu.CompilerParams(vmem_limit_bytes=40 * 2**20),
        cost_estimate=pl.CostEstimate(
            flops=4 * groups * rows * cols * head_size * 2,
            bytes_accessed=8 * tokens_all * head_size,
            transcendentals=groups * rows * cols,
        ),
    )(query_tiles, key_tiles, query_unit, key_unit, value_unit, bias)


def unit_backward(query_unit, key_unit, value_unit, out_unit, log_unit, grad_unit, tables, tile_len):
    query_tiles, key_tiles, bias = tables
    tokens_all, head_size = query_unit.shape
    groups, group_size = query_tiles.shape
    rows, cols = key_tiles.shape[1] * tile_len, group_size * tile_len
    whole = whole_spec((tokens_all, head_size))
    shape = jax.ShapeDtypeStruct((tokens_all, head_size), jnp.bfloat16)
    return pl.pallas_call(
        functools.partial(backward_kernel, tile_len),
        out_shape=(shape, shape, shape),
        grid_spec=pltpu.PrefetchScalarGridSpec(
            num_scalar_prefetch=2,
            grid=(groups,),
            in_specs=[whole] * 5 + [group_spec(bias.shape[1:]), group_spec((1, cols))],
            out_specs=(whole, whole, whole),
            scratch_shapes=[
                pltpu.VMEM((cols, head_size), jnp.bfloat16),
                pltpu.VMEM((rows, head_size), jnp.bfloat16),
                pltpu.VMEM((rows, head_size), jnp.bfloat16),
                pltpu.VMEM((cols, head_size), jnp.bfloat16),
                pltpu.VMEM((cols, head_size), jnp.bfloat16),
                pltpu.VMEM((tokens_all, head_size), jnp.float32),
                pltpu.VMEM((tokens_all, head_size), jnp.float32),
            ],
        ),
        compiler_params=pltpu.CompilerParams(vmem_limit_bytes=48 * 2**20),
        cost_estimate=pl.CostEstimate(
            flops=10 * groups * rows * cols * head_size * 2,
            bytes_accessed=16 * tokens_all * head_size,
            transcendentals=groups * rows * cols,
        ),
    )(query_tiles, key_tiles, query_unit, key_unit, value_unit, out_unit, grad_unit, bias, log_unit)


def local(queries, keys_in, values_in, pair_keys, out_weight, cotangent):
    tok_rows, local_videos, head_count, head_size = queries.shape
    unit_total = local_videos * head_count
    seq_size = lax.axis_size("seq")
    units_here = unit_total // seq_size
    row_count = tok_rows * local_videos
    width_heads = head_count * head_size
    split_shape = (tok_rows, seq_size, units_here, head_size)
    query_all = lax.all_to_all(
        queries.reshape(split_shape), "seq", split_axis=1, concat_axis=0, tiled=True
    )
    key_all = lax.all_to_all(
        keys_in.reshape(split_shape), "seq", split_axis=1, concat_axis=0, tiled=True
    )
    value_all = lax.all_to_all(
        values_in.reshape(split_shape), "seq", split_axis=1, concat_axis=0, tiled=True
    )
    tile_len = query_all.shape[0] // pair_keys.shape[0]
    tables = group_tables(pair_keys, tile_len)
    query_unit, key_unit, value_unit = query_all[:, 0, 0], key_all[:, 0, 0], value_all[:, 0, 0]
    cot_rows = cotangent.reshape(row_count, cotangent.shape[2])
    weight_cols = lax.all_gather(out_weight, "dp", axis=1, tiled=True)
    pair = [(index, index ^ 1) for index in range(seq_size)]
    parity_groups = [list(range(core, seq_size, 2)) for core in range(2)]
    core = lax.axis_index("seq") % 2
    own_rows = weight_cols.shape[0]
    weight_mine = lax.all_gather(
        weight_cols, "seq", axis=0, tiled=True, axis_index_groups=parity_groups
    )
    weight_other = lax.ppermute(weight_mine, "seq", pair)
    mine_split = weight_mine.reshape(seq_size // 2, 1, own_rows, -1)
    other_split = weight_other.reshape(seq_size // 2, 1, own_rows, -1)
    is_mine = (jnp.arange(2, dtype=jnp.int32) == core).reshape(1, 2, 1, 1)
    weight_full = jnp.where(is_mine, mine_split, other_split).reshape(width_heads, -1)
    cot_pair = jnp.concatenate((cot_rows, lax.ppermute(cot_rows, "seq", pair)), axis=0)
    grad_attention = jnp.einsum(
        "rd,cd->rc", cot_rows, weight_full, preferred_element_type=jnp.float32
    ).astype(jnp.bfloat16)
    query_unit, grad_attention = lax.optimization_barrier((query_unit, grad_attention))
    grad_heads = lax.all_to_all(
        grad_attention.reshape(split_shape), "seq", split_axis=1, concat_axis=0, tiled=True
    )
    result, log_total = unit_forward(query_unit, key_unit, value_unit, tables, tile_len)
    result, grad_heads = lax.optimization_barrier((result, grad_heads))
    heads_out = result[:, None, None]
    attn_tok = lax.all_to_all(heads_out, "seq", split_axis=0, concat_axis=1, tiled=True)
    attn_rows = attn_tok.reshape(row_count, width_heads)
    projected = jnp.dot(attn_rows, weight_full, preferred_element_type=jnp.float32)
    output = projected.astype(jnp.bfloat16).reshape(tok_rows, local_videos, cotangent.shape[2])
    attn_split = attn_rows.reshape(row_count, seq_size // 2, 2, own_rows)
    attn_even = attn_split[:, :, 0].reshape(row_count, -1)
    attn_odd = attn_split[:, :, 1].reshape(row_count, -1)
    attn_keep = jnp.where(core == 0, attn_even, attn_odd)
    attn_give = jnp.where(core == 0, attn_odd, attn_even)
    attn_pair = jnp.concatenate((attn_keep, lax.ppermute(attn_give, "seq", pair)), axis=0)
    by_rows = lax.psum_scatter(
        jnp.einsum("rc,rd->cd", attn_pair, cot_pair, preferred_element_type=jnp.float32).astype(
            jnp.bfloat16
        ),
        "seq",
        scatter_dimension=0,
        axis_index_groups=parity_groups,
        tiled=True,
    )
    weight_grad = lax.psum_scatter(by_rows, "dp", scatter_dimension=1, tiled=True).astype(
        jnp.float32
    )
    grad_q, grad_k, grad_v = unit_backward(
        query_unit, key_unit, value_unit, result, log_total, grad_heads[:, 0, 0], tables, tile_len
    )
    query_parts = [grad_q]
    key_parts = [grad_k]
    value_parts = [grad_v]
    grad_query_tok, grad_key_tok, grad_value_tok = (
        lax.all_to_all(
            jnp.stack(query_parts, 1)[:, None], "seq", split_axis=0, concat_axis=1, tiled=True
        ),
        lax.all_to_all(
            jnp.stack(key_parts, 1)[:, None], "seq", split_axis=0, concat_axis=1, tiled=True
        ),
        lax.all_to_all(
            jnp.stack(value_parts, 1)[:, None], "seq", split_axis=0, concat_axis=1, tiled=True
        ),
    )
    full_shape = (tok_rows, local_videos, head_count, head_size)
    return (
        output,
        grad_query_tok.reshape(full_shape),
        grad_key_tok.reshape(full_shape),
        grad_value_tok.reshape(full_shape),
        weight_grad,
    )


def solution(mesh):
    placed = (
        P("seq", "dp", None, None),
        P("seq", "dp", None, None),
        P("seq", "dp", None, None),
        P(),
        P("seq", "dp"),
        P("seq", "dp", None),
    )
    return jax.shard_map(
        local,
        mesh=mesh,
        in_specs=placed,
        out_specs=(
            P("seq", "dp", None),
            P("seq", "dp", None, None),
            P("seq", "dp", None, None),
            P("seq", "dp", None, None),
            P("seq", "dp"),
        ),
        check_vma=False,
    )
```

```python
import functools

import jax
import jax.numpy as jnp
from jax import lax
from jax.experimental import pallas as pl
from jax.experimental.pallas import tpu as pltpu
from jax.sharding import PartitionSpec as P


LOG2E = 1.4426950408889634
HIDDEN = -1e30
CHUNK_TILES = 4


def group_tables(pair_keys, tile_len):
    tile_count, slot_count = pair_keys.shape
    group_count = 8
    group_size = 8
    padded = -(-slot_count // CHUNK_TILES) * CHUNK_TILES
    tile_ids = jnp.arange(tile_count, dtype=jnp.int32)
    counts = jnp.sum((pair_keys >= 0).astype(jnp.int32), axis=1)
    is_corner = counts == group_size
    before = (tile_ids[None, :] < tile_ids[:, None]) & is_corner[None, :]
    rank = jnp.sum(before.astype(jnp.int32), axis=1)
    pick = (rank[None, :] == jnp.arange(group_count, dtype=jnp.int32)[:, None]) & is_corner[None, :]
    query_tiles = jnp.sum(jnp.where(pick[:, :, None], pair_keys[None, :, :group_size], 0), axis=1)
    member = query_tiles[:, :, None] == tile_ids[None, None, :]
    inner = jnp.any(member, axis=1) & (counts == slot_count)[None, :]
    key_tiles = jnp.sum(jnp.where(inner[:, :, None], pair_keys[None], 0), axis=1)
    rows = jnp.sum(jnp.where(member[..., None], pair_keys[None, None], 0), axis=2)
    seen = jnp.any(rows[:, None, :, :] == key_tiles[:, :, None, None], axis=3)
    bias = jnp.where(seen, 0.0, HIDDEN).astype(jnp.float32)
    bias = jnp.pad(bias, ((0, 0), (0, padded - slot_count), (0, 0)), constant_values=HIDDEN)
    bias = jnp.repeat(bias, tile_len, axis=2)
    key_tiles = jnp.pad(key_tiles, ((0, 0), (0, padded - slot_count)))
    return query_tiles, key_tiles, bias


def gather_tiles(table, group, source, target, count, tile_len):
    for slot in range(count):
        start = pl.multiple_of(table[group, slot] * tile_len, tile_len)
        target[slot * tile_len : (slot + 1) * tile_len, :] = source[pl.ds(start, tile_len), :]


def dot_nt(left, right):
    return lax.dot_general(
        left, right, (((1,), (1,)), ((), ())), preferred_element_type=jnp.float32
    )


def dot_tn(left, right):
    return lax.dot_general(
        left, right, (((0,), (0,)), ((), ())), preferred_element_type=jnp.float32
    )


def add_bias(scores, bias_rows, tile_len):
    keys, cols = scores.shape
    split = scores.reshape(keys // tile_len, tile_len, cols) + bias_rows[:, None, :]
    return split.reshape(keys, cols)


def forward_kernel(
    tile_len, q_table, k_table, q_ref, k_ref, v_ref, bias_ref, o_ref, lse_ref,
    q_buf, k_buf, v_buf, s_buf,
):
    group = pl.program_id(0)
    query_count = q_buf.shape[0] // tile_len
    key_count = k_buf.shape[0] // tile_len
    gather_tiles(q_table, group, q_ref, q_buf, query_count, tile_len)
    gather_tiles(k_table, group, k_ref, k_buf, key_count, tile_len)
    gather_tiles(k_table, group, v_ref, v_buf, key_count, tile_len)
    head_size = q_buf.shape[1]
    factor = head_size ** (-0.5) * LOG2E
    step = CHUNK_TILES * tile_len
    chunks = key_count // CHUNK_TILES
    queries = q_buf[...]
    top = None
    for part in range(chunks):
        scores = dot_nt(k_buf[part * step : (part + 1) * step, :], queries) * factor
        bias_rows = bias_ref[0, part * CHUNK_TILES : (part + 1) * CHUNK_TILES, :]
        scores = add_bias(scores, bias_rows, tile_len)
        s_buf[part * step : (part + 1) * step, :] = scores
        part_top = jnp.max(scores, axis=0, keepdims=True)
        top = part_top if top is None else jnp.maximum(top, part_top)
    total = jnp.zeros_like(top)
    result = jnp.zeros((head_size, queries.shape[0]), jnp.float32)
    for part in range(chunks):
        probs = jnp.exp2(s_buf[part * step : (part + 1) * step, :] - top)
        total = total + jnp.sum(probs, axis=0, keepdims=True)
        values = v_buf[part * step : (part + 1) * step, :]
        result = result + dot_tn(values, probs.astype(jnp.bfloat16))
    lse_ref[0] = top + jnp.log2(total)
    out = jnp.transpose(result / total).astype(jnp.bfloat16)
    for slot in range(query_count):
        start = pl.multiple_of(q_table[group, slot] * tile_len, tile_len)
        o_ref[pl.ds(start, tile_len), :] = out[slot * tile_len : (slot + 1) * tile_len, :]


def backward_kernel(
    tile_len, q_table, k_table, q_ref, k_ref, v_ref, o_ref, g_ref, bias_ref, lse_ref,
    dq_ref, dk_ref, dv_ref, q_buf, k_buf, v_buf, o_buf, g_buf, k_acc, v_acc,
):
    group = pl.program_id(0)
    query_count = q_buf.shape[0] // tile_len
    key_count = k_buf.shape[0] // tile_len

    @pl.when(group == 0)
    def _():
        k_acc[...] = jnp.zeros_like(k_acc)
        v_acc[...] = jnp.zeros_like(v_acc)

    gather_tiles(q_table, group, q_ref, q_buf, query_count, tile_len)
    gather_tiles(q_table, group, o_ref, o_buf, query_count, tile_len)
    gather_tiles(q_table, group, g_ref, g_buf, query_count, tile_len)
    gather_tiles(k_table, group, k_ref, k_buf, key_count, tile_len)
    gather_tiles(k_table, group, v_ref, v_buf, key_count, tile_len)
    head_size = q_buf.shape[1]
    scale = head_size ** (-0.5)
    step = CHUNK_TILES * tile_len
    chunks = key_count // CHUNK_TILES
    queries = q_buf[...]
    grads = g_buf[...]
    products = grads.astype(jnp.float32) * o_buf[...].astype(jnp.float32)
    delta = jnp.sum(jnp.transpose(products), axis=0, keepdims=True)
    log_total = lse_ref[0]
    query_grad = jnp.zeros((head_size, queries.shape[0]), jnp.float32)
    for part in range(chunks):
        keys = k_buf[part * step : (part + 1) * step, :]
        values = v_buf[part * step : (part + 1) * step, :]
        bias_rows = bias_ref[0, part * CHUNK_TILES : (part + 1) * CHUNK_TILES, :] - log_total
        scores = dot_nt(keys, queries) * (scale * LOG2E)
        probs = jnp.exp2(add_bias(scores, bias_rows, tile_len))
        grad_probs = dot_nt(values, grads)
        grad_scores = (probs * ((grad_probs - delta) * scale)).astype(jnp.bfloat16)
        value_part = jnp.dot(
            probs.astype(jnp.bfloat16), grads, preferred_element_type=jnp.float32
        )
        key_part = jnp.dot(grad_scores, queries, preferred_element_type=jnp.float32)
        query_grad = query_grad + dot_tn(keys, grad_scores)
        for slot in range(CHUNK_TILES):
            tile = k_table[group, part * CHUNK_TILES + slot]
            start = pl.multiple_of(tile * tile_len, tile_len)
            here = slice(slot * tile_len, (slot + 1) * tile_len)
            k_acc[pl.ds(start, tile_len), :] += key_part[here, :]
            v_acc[pl.ds(start, tile_len), :] += value_part[here, :]
    out = jnp.transpose(query_grad).astype(jnp.bfloat16)
    for slot in range(query_count):
        start = pl.multiple_of(q_table[group, slot] * tile_len, tile_len)
        dq_ref[pl.ds(start, tile_len), :] = out[slot * tile_len : (slot + 1) * tile_len, :]

    @pl.when(group == pl.num_programs(0) - 1)
    def _():
        dk_ref[...] = k_acc[...].astype(jnp.bfloat16)
        dv_ref[...] = v_acc[...].astype(jnp.bfloat16)


def whole_spec(shape):
    return pl.BlockSpec(shape, lambda group, q_table, k_table: (0, 0))


def group_spec(shape):
    return pl.BlockSpec((1,) + shape, lambda group, q_table, k_table: (group, 0, 0))


def unit_forward(query_unit, key_unit, value_unit, tables, tile_len):
    query_tiles, key_tiles, bias = tables
    tokens_all, head_size = query_unit.shape
    groups, group_size = query_tiles.shape
    rows, cols = key_tiles.shape[1] * tile_len, group_size * tile_len
    whole = whole_spec((tokens_all, head_size))
    return pl.pallas_call(
        functools.partial(forward_kernel, tile_len),
        out_shape=(
            jax.ShapeDtypeStruct((tokens_all, head_size), jnp.bfloat16),
            jax.ShapeDtypeStruct((groups, 1, cols), jnp.float32),
        ),
        grid_spec=pltpu.PrefetchScalarGridSpec(
            num_scalar_prefetch=2,
            grid=(groups,),
            in_specs=[whole, whole, whole, group_spec(bias.shape[1:])],
            out_specs=(whole, group_spec((1, cols))),
            scratch_shapes=[
                pltpu.VMEM((cols, head_size), jnp.bfloat16),
                pltpu.VMEM((rows, head_size), jnp.bfloat16),
                pltpu.VMEM((rows, head_size), jnp.bfloat16),
                pltpu.VMEM((rows, cols), jnp.float32),
            ],
        ),
        compiler_params=pltpu.CompilerParams(vmem_limit_bytes=40 * 2**20),
        cost_estimate=pl.CostEstimate(
            flops=4 * groups * rows * cols * head_size * 2,
            bytes_accessed=8 * tokens_all * head_size,
            transcendentals=groups * rows * cols,
        ),
    )(query_tiles, key_tiles, query_unit, key_unit, value_unit, bias)


def unit_backward(query_unit, key_unit, value_unit, out_unit, log_unit, grad_unit, tables, tile_len):
    query_tiles, key_tiles, bias = tables
    tokens_all, head_size = query_unit.shape
    groups, group_size = query_tiles.shape
    rows, cols = key_tiles.shape[1] * tile_len, group_size * tile_len
    whole = whole_spec((tokens_all, head_size))
    shape = jax.ShapeDtypeStruct((tokens_all, head_size), jnp.bfloat16)
    return pl.pallas_call(
        functools.partial(backward_kernel, tile_len),
        out_shape=(shape, shape, shape),
        grid_spec=pltpu.PrefetchScalarGridSpec(
            num_scalar_prefetch=2,
            grid=(groups,),
            in_specs=[whole] * 5 + [group_spec(bias.shape[1:]), group_spec((1, cols))],
            out_specs=(whole, whole, whole),
            scratch_shapes=[
                pltpu.VMEM((cols, head_size), jnp.bfloat16),
                pltpu.VMEM((rows, head_size), jnp.bfloat16),
                pltpu.VMEM((rows, head_size), jnp.bfloat16),
                pltpu.VMEM((cols, head_size), jnp.bfloat16),
                pltpu.VMEM((cols, head_size), jnp.bfloat16),
                pltpu.VMEM((tokens_all, head_size), jnp.float32),
                pltpu.VMEM((tokens_all, head_size), jnp.float32),
            ],
        ),
        compiler_params=pltpu.CompilerParams(vmem_limit_bytes=48 * 2**20),
        cost_estimate=pl.CostEstimate(
            flops=10 * groups * rows * cols * head_size * 2,
            bytes_accessed=16 * tokens_all * head_size,
            transcendentals=groups * rows * cols,
        ),
    )(query_tiles, key_tiles, query_unit, key_unit, value_unit, out_unit, grad_unit, bias, log_unit)


def local(queries, keys_in, values_in, pair_keys, out_weight, cotangent):
    tok_rows, local_videos, head_count, head_size = queries.shape
    unit_total = local_videos * head_count
    seq_size = lax.axis_size("seq")
    units_here = unit_total // seq_size
    row_count = tok_rows * local_videos
    width_heads = head_count * head_size
    split_shape = (tok_rows, seq_size, units_here, head_size)
    query_all = lax.all_to_all(
        queries.reshape(split_shape), "seq", split_axis=1, concat_axis=0, tiled=True
    )
    key_all = lax.all_to_all(
        keys_in.reshape(split_shape), "seq", split_axis=1, concat_axis=0, tiled=True
    )
    cot_rows = cotangent.reshape(row_count, cotangent.shape[2])
    weight_cols = lax.all_gather(out_weight, "dp", axis=1, tiled=True)
    weight_full = lax.all_gather(weight_cols, "seq", axis=0, tiled=True)
    query_all, key_all, values_in, weight_full = lax.optimization_barrier(
        (query_all, key_all, values_in, weight_full)
    )
    value_all = lax.all_to_all(
        values_in.reshape(split_shape), "seq", split_axis=1, concat_axis=0, tiled=True
    )
    tile_len = query_all.shape[0] // pair_keys.shape[0]
    tables = group_tables(pair_keys, tile_len)
    query_unit, key_unit, value_unit = query_all[:, 0, 0], key_all[:, 0, 0], value_all[:, 0, 0]
    grad_attention = jnp.einsum(
        "rd,cd->rc", cot_rows, weight_full, preferred_element_type=jnp.float32
    ).astype(jnp.bfloat16)
    query_unit, grad_attention = lax.optimization_barrier((query_unit, grad_attention))
    grad_heads = lax.all_to_all(
        grad_attention.reshape(split_shape), "seq", split_axis=1, concat_axis=0, tiled=True
    )
    result, log_total = unit_forward(query_unit, key_unit, value_unit, tables, tile_len)
    result, grad_heads = lax.optimization_barrier((result, grad_heads))
    heads_out = result[:, None, None]
    attn_tok = lax.all_to_all(heads_out, "seq", split_axis=0, concat_axis=1, tiled=True)
    attn_rows = attn_tok.reshape(row_count, width_heads)
    projected = jnp.dot(attn_rows, weight_full, preferred_element_type=jnp.float32)
    output = projected.astype(jnp.bfloat16).reshape(tok_rows, local_videos, cotangent.shape[2])
    by_rows = lax.psum_scatter(
        jnp.einsum("rc,rd->cd", attn_rows, cot_rows, preferred_element_type=jnp.float32).astype(
            jnp.bfloat16
        ),
        "seq",
        scatter_dimension=0,
        tiled=True,
    )
    weight_grad = lax.psum_scatter(by_rows, "dp", scatter_dimension=1, tiled=True).astype(
        jnp.float32
    )
    grad_q, grad_k, grad_v = unit_backward(
        query_unit, key_unit, value_unit, result, log_total, grad_heads[:, 0, 0], tables, tile_len
    )
    query_parts = [grad_q]
    key_parts = [grad_k]
    value_parts = [grad_v]
    grad_query_tok, grad_key_tok, grad_value_tok = (
        lax.all_to_all(
            jnp.stack(query_parts, 1)[:, None], "seq", split_axis=0, concat_axis=1, tiled=True
        ),
        lax.all_to_all(
            jnp.stack(key_parts, 1)[:, None], "seq", split_axis=0, concat_axis=1, tiled=True
        ),
        lax.all_to_all(
            jnp.stack(value_parts, 1)[:, None], "seq", split_axis=0, concat_axis=1, tiled=True
        ),
    )
    full_shape = (tok_rows, local_videos, head_count, head_size)
    return (
        output,
        grad_query_tok.reshape(full_shape),
        grad_key_tok.reshape(full_shape),
        grad_value_tok.reshape(full_shape),
        weight_grad,
    )


def solution(mesh):
    placed = (
        P("seq", "dp", None, None),
        P("seq", "dp", None, None),
        P("seq", "dp", None, None),
        P(),
        P("seq", "dp"),
        P("seq", "dp", None),
    )
    return jax.shard_map(
        local,
        mesh=mesh,
        in_specs=placed,
        out_specs=(
            P("seq", "dp", None),
            P("seq", "dp", None, None),
            P("seq", "dp", None, None),
            P("seq", "dp", None, None),
            P("seq", "dp"),
        ),
        check_vma=False,
    )
```
